256 devices in a mesh: replica: 4 (over z_hi), fsdp: 8 (over x, core), tensor: 8 (over y, z_lo).
Axes of the slice: x: 4, y: 4, z: 8 (z_hi: 4, z_lo: 2; z = z_hi * 2 + z_lo), core: 2. Of those that a mesh axis runs over, the one named last changes fastest.
Arguments:
- residual: bfloat16 [8192, 8192], P(('replica', 'fsdp'), 'tensor'), may hold values from -0.6 to 0.6
- norm_gain: bfloat16 [8192], P('tensor'), may hold values from 0.25 to 3.5
- kv_weight: bfloat16 [4, 8192, 6144], P('replica', 'fsdp', 'tensor'), may hold values from -0.0625 to 0.0625
- kv_cotangent: bfloat16 [8192, 6144], P(('replica', 'fsdp'), 'tensor'), may hold values from -0.19921875 to 0.19921875
- frag_local: bfloat16 [4, 8192, 2048], P('replica', 'fsdp', 'tensor'), may hold values from -6 to 6
- frag_base: bfloat16 [8192, 2048], P('fsdp', 'tensor'), may hold values from -6 to 6
- frag_moment: float32 [8192, 2048], P('fsdp', 'tensor'), may hold values from -3 to 3
Outputs:
- residual_grad: bfloat16 [8192, 8192], P(('replica', 'fsdp'), 'tensor')
- kv_weight_grad: float32 [4, 8192, 6144], P('replica', 'fsdp', 'tensor')
- frag_new: bfloat16 [8192, 2048], P('fsdp', 'tensor')
- moment_new: float32 [8192, 2048], P('fsdp', 'tensor')
The draws below stay inside these ranges and needn't reach their ends.
All inputs are finite; a program needn't handle non-finite values. Where the reference program divides by a largest or mean magnitude, that divisor is 1e-20 or more.
Results may differ from the reference program's by a relative error of at most 0.019.
Values may be sent and summed in bfloat16 or wider, within the bound.
A program may use at most 128 MiB of HBM per device.

```python
import math
import jax
import jax.numpy as jnp
from jax import lax

D = 8192
QKV = 6144
KV = 2048
BLOCK = 128
TOK_DEV = 256
REPLICAS = 4
TOKENS = 8192
N_REPLICA = 4
N_FSDP = 8
N_TENSOR = 8


def rising_scale(key, top):
    position = jnp.arange(D, dtype=jnp.float32) / (D - 1)
    jitter = jax.random.uniform(key, (D,), jnp.float32, 0.7, 1.3)
    spread = math.sqrt((top * top - 1.0) / (2.0 * math.log(top)))
    return jnp.exp(position * math.log(top)) * jitter / spread


def draw_residual(key, part):
    key = jax.random.fold_in(key, 11)
    first, second = jax.random.split(key)
    top = 10.0
    values = jnp.clip(jax.random.normal(first, (TOKENS, D), jnp.float32), -4.0, 4.0)
    scale = 0.05 * rising_scale(second, top)
    return (values * scale[None, :]).astype(jnp.bfloat16)


def draw_norm_gain(key, part):
    key = jax.random.fold_in(key, 23)
    lower, upper = (0.5, 2.0)
    position = jnp.arange(D, dtype=jnp.float32) / (D - 1)
    jitter = jax.random.uniform(key, (D,), jnp.float32, 0.8, 1.2)
    return (lower * jnp.exp(position * math.log(upper / lower)) * jitter).astype(jnp.bfloat16)


def level_of(key, shape, pieces, smallest, high):
    loudness = 1.0
    for dim, shards_of in pieces:
        steps = jax.random.uniform(jax.random.fold_in(jax.random.fold_in(key, 6), dim), (shards_of,), jnp.float32, smallest / len(pieces), high / len(pieces))
        loudness = loudness * jnp.repeat(jnp.exp(steps), shape[dim] // shards_of).reshape((-1,) + (1,) * (len(shape) - 1 - dim))
    return loudness


def noise(rng, extent, scale, reach, pieces=(), held_as=jnp.bfloat16):
    result = scale * jax.random.normal(rng, extent, jnp.float32)
    if pieces:
        result = result * level_of(rng, extent, pieces, -0.22, 0.18)
    return jnp.clip(result, -reach, reach).astype(held_as)


def setup_inputs(seed: int = 0) -> dict:
    key_of = jax.random.split(jax.random.key(seed), 8)
    residual = draw_residual(jax.random.fold_in(key_of[7], 71), 0)
    norm_gain = draw_norm_gain(jax.random.fold_in(key_of[7], 71), 0)
    kv_weight = noise(key_of[2], (REPLICAS, D, QKV), D ** -0.5, 0.0625, ((0, 4), (1, 8), (2, 8)))
    kv_cotangent = noise(key_of[3], (TOKENS, QKV), 0.03, 0.19921875, ((0, 32), (1, 8)))
    frag_local = noise(key_of[4], (REPLICAS, D, KV), 1.0, 6.0, ((0, 4), (1, 8), (2, 8)))
    frag_base = noise(key_of[5], (D, KV), 1.0, 6.0, ((0, 8), (1, 8)))
    frag_moment = noise(key_of[6], (D, KV), 0.5, 3.0, ((0, 8), (1, 8)), jnp.float32)
    return {"residual": residual, "norm_gain": norm_gain, "kv_weight": kv_weight, "kv_cotangent": kv_cotangent, "frag_local": frag_local, "frag_base": frag_base, "frag_moment": frag_moment}


def reference(residual, norm_gain, kv_weight, kv_cotangent, frag_local, frag_base, frag_moment):
    eps = 1e-05
    per_replica = TOK_DEV * N_FSDP
    kv_local = QKV // N_TENSOR
    xf = residual.astype(jnp.float32)
    rinv = lax.rsqrt(lax.optimization_barrier(jnp.mean(xf * xf, axis=-1, keepdims=True)) + eps)
    normalized = xf * rinv
    gain = norm_gain.astype(jnp.float32)
    normed = (normalized * gain).astype(jnp.bfloat16)
    grads_rows = []
    weight_grads = []
    for rep in range(N_REPLICA):
        lo = rep * per_replica
        h_rows = normed[lo:lo + per_replica]
        d_rows = kv_cotangent[lo:lo + per_replica]
        weights = kv_weight[rep]
        total = jnp.zeros((per_replica, D), jnp.float32)
        for group in range(N_TENSOR):
            cols = slice(group * kv_local, (group + 1) * kv_local)
            part = lax.dot_general(d_rows[:, cols], weights[:, cols], (((1,), (1,)), ((), ())), preferred_element_type=jnp.float32)
            total = total + part.astype(jnp.bfloat16).astype(jnp.float32)
        grads_rows.append(total)
        wsum = jnp.zeros((D, QKV), jnp.float32)
        for group in range(N_FSDP):
            rows = slice(group * TOK_DEV, (group + 1) * TOK_DEV)
            part = lax.dot_general(h_rows[rows], d_rows[rows], (((0,), (0,)), ((), ())), preferred_element_type=jnp.float32)
            wsum = wsum + part.astype(jnp.bfloat16).astype(jnp.float32)
        weight_grads.append(wsum)
    normed_grad = jnp.concatenate(grads_rows, axis=0)
    scaled_grad = gain * normed_grad
    inner = lax.optimization_barrier(jnp.mean(scaled_grad * normalized, axis=-1, keepdims=True))
    residual_grad = (rinv * (scaled_grad - normalized * inner)).astype(jnp.bfloat16)
    kv_weight_grad = jnp.stack(weight_grads, axis=0)
    base = frag_base.astype(jnp.float32)
    delta = base[None] - frag_local.astype(jnp.float32)
    blocks = delta.reshape(N_REPLICA, D, KV // BLOCK, BLOCK)
    scales = (lax.optimization_barrier(jnp.max(jnp.abs(blocks), axis=-1, keepdims=True)) + 1e-06).astype(jnp.bfloat16)
    codes = (blocks / scales.astype(jnp.float32)).astype(jnp.bfloat16)
    summed = lax.optimization_barrier(jnp.sum(codes.astype(jnp.float32) * scales.astype(jnp.float32), axis=0))
    outer_grad = (summed / N_REPLICA).reshape(D, KV)
    moment_new = 0.9 * frag_moment + outer_grad
    frag_new = (base - 0.7 * (outer_grad + 0.9 * moment_new)).astype(jnp.bfloat16)
    return (residual_grad, kv_weight_grad, frag_new, moment_new)
```

```python
import jax
import jax.numpy as jnp
from jax import lax
from jax.experimental import pallas as pl
from jax.experimental.pallas import tpu as pltpu
from jax.sharding import PartitionSpec as P

D = 8192
BLOCK = 128
EPS = 1e-05
TOK = 256
FEAT = 1024
COLS = 768
HALF = FEAT // 2
ROWS = 128
QROWS = 256
F32 = jnp.float32
BF = jnp.bfloat16
MESH = pl.DeviceIdType.MESH
NSEND = 100


def lanes(v):
    out = v[:, :128]
    for i in range(1, v.shape[1] // 128):
        out = out + v[:, i * 128 : (i + 1) * 128]
    return out


def kernel(
    res_hbm, gain_ref, w_hbm, cot_hbm, loc_hbm, base_hbm,
    rg_ref, dw_hbm, fo_hbm,
    res, cot, loc, base, xg, pn, wv, ct, po, ps, pr, cs, cr, ng, dw, dws,
    sq, rcol, sums, inns, fq, fr, fs,
    lsem, ssem, r_sum, r_inn, r_pn, r_pd, r_w, r_ct, r_pr, r_cr, r_ng, r_dw, r_fr, r_fo,
):
    r = lax.axis_index("replica")
    f = lax.axis_index("fsdp")
    t = lax.axis_index("tensor")
    x, c = lax.div(f, 2), lax.rem(f, 2)
    y, zl = lax.div(t, 2), lax.rem(t, 2)

    def dev(x_, c_, y_, z_, r_=r):
        return (r_, x_ * 2 + c_, y_ * 2 + z_)

    def ring(v, o):
        return lax.rem(v + o, 4)

    sib = dev(x, 1 - c, y, zl)
    swap = dev(x, 1 - c, y, 1 - zl)
    up, down = dev(x, c, ring(y, 1), zl), dev(x, c, ring(y, 3), zl)
    xup, xdown, xfar = (dev(ring(x, o), c, y, zl) for o in (1, 3, 2))
    tensors = [(r, f, lax.rem(t + o, 8)) for o in range(1, 8)]
    replicas = [(ring(r, o), f, t) for o in (1, 2, 3)]
    d = ring(y - x + 4, 0)
    straight = c == zl
    crossed = c != zl

    barrier = pltpu.get_barrier_semaphore()
    peers = tensors + replicas + [sib, swap, xup, xdown, xfar]
    for peer in peers:
        pl.semaphore_signal(barrier, inc=1, device_id=peer, device_id_type=MESH)

    loads = [
        pltpu.make_async_copy(src, dst, lsem.at[i])
        for i, (src, dst) in enumerate(((res_hbm, res), (cot_hbm, cot), (loc_hbm, loc), (base_hbm, base)))
    ]
    for load in loads:
        load.start()

    sends = []

    def make(src, dst, sem, device, pred=None):
        cp = pltpu.make_async_remote_copy(
            src_ref=src, dst_ref=dst, send_sem=ssem.at[len(sends)], recv_sem=sem, device_id=device, device_id_type=MESH
        )
        sends.append((pred, cp))
        return cp

    def send(src, dst, sem, device, pred=None):
        cp = make(src, dst, sem, device, pred)
        if pred is None:
            cp.start()
        else:
            pl.when(pred)(cp.start)

    def arrive(ref, sem):
        pltpu.make_async_remote_copy(
            src_ref=ref, dst_ref=ref, send_sem=ssem.at[0], recv_sem=sem, device_id=sib, device_id_type=MESH
        ).wait_recv()

    gain = gain_ref[...].astype(F32)

    loads[0].wait()

    def scale_rows(i, _):
        rows = pl.ds(pl.multiple_of(i * 32, 32), 32)
        v = res[rows, :].astype(F32)
        g = (v * gain).astype(BF)
        xg[0, rows, :] = g[:, :HALF]
        xg[1, rows, :] = g[:, HALF:]
        sq[rows, :] = lanes(v * v)
        return 0

    lax.fori_loop(0, TOK // 32, scale_rows, 0)
    sums[t] = jnp.broadcast_to(jnp.sum(sq[...].T, axis=0, keepdims=True), (8, TOK))

    pl.semaphore_wait(barrier, len(peers))

    for peer in tensors:
        send(sums.at[t], sums.at[t], r_sum.at[t], peer)

    def slot(k):
        return ring(x, (0, 1, 3, 2)[k])

    for q in range(2):
        for h in range(2):
            rows = pl.ds(h * ROWS, ROWS)
            send(xg.at[q, rows], pn.at[x, q, c, rows], r_pn.at[x, q, h], dev(y, c, y, zl), d != 0)

    @pl.when(d == 0)
    def _():
        for q in range(2):
            pn[x, q, c] = xg[q]

    bcast = {}
    for j in range(8):
        xs, q = slot(j // 2), j % 2
        for h in range(2):
            ref = pn.at[xs, q, c, pl.ds(h * ROWS, ROWS)]
            bcast[j, h] = (
                make(ref, ref, r_pn.at[xs, q, h], (up, down)[h], d != (3, 1)[h]),
                lambda ref=ref, xs=xs, q=q, h=h: arrive(ref, r_pn.at[xs, q, h]),
            )

    def b_step(s):
        if s < 8:
            @pl.when(d == 0)
            def _():
                for h in range(2):
                    if s >= 2:
                        bcast[s, h][1]()
                    bcast[s, h][0].start()
        if 0 <= s - 1 < 8:
            for h in range(2):
                @pl.when(d == (1, 3)[h])
                def _():
                    bcast[s - 1, h][1]()
                    bcast[s - 1, h][0].start()
        if 0 <= s - 2 < 8:
            @pl.when(d == 2)
            def _():
                for h in range(2):
                    bcast[s - 2, h][1]()
                    bcast[s - 2, h][0].start()
        if 0 <= s - 3 < 8:
            for h in range(2):
                @pl.when(d == (3, 1)[h])
                def _():
                    bcast[s - 3, h][1]()
            j = s - 3
            ref = pn.at[slot(j // 2), j % 2, c]
            send(ref, ref, r_pd.at[slot(j // 2), j % 2], sib)

    def w_send(q):
        rows = pl.ds(q * HALF, HALF)
        send(w_hbm.at[rows], wv.at[q], r_w.at[q], swap, crossed)

    w_own = [pltpu.make_async_copy(w_hbm.at[pl.ds(q * HALF, HALF)], wv.at[q], r_w.at[q]) for q in range(2)]

    @pl.when(straight)
    def _():
        for q in range(2):
            w_own[q].start()

    b_step(0)
    b_step(1)
    w_send(0)

    loads[1].wait()
    for o in range(1, 8):
        other = lax.rem(t + o, 8)
        arrive(sums.at[other], r_sum.at[other])
    total = jnp.sum(sums[...], axis=0)[0:1]
    rinv = lax.rsqrt(total / D + EPS)
    rcol[...] = jnp.broadcast_to(rinv, (128, TOK)).T

    def scale_cot(i, _):
        rows = pl.ds(pl.multiple_of(i * 32, 32), 32)
        by = rcol[rows, :]
        for l in range(COLS // 128):
            span = slice(l * 128, (l + 1) * 128)
            cot[rows, span] = (cot[rows, span].astype(F32) * by).astype(BF)
        return 0

    lax.fori_loop(0, TOK // 32, scale_cot, 0)
    send(cot, ct.at[x, c], r_ct.at[x, c], dev(x, zl, y, 1 - zl))
    send(cot, ct.at[x, c], r_ct.at[x, c], sib, crossed)

    @pl.when(straight)
    def _():
        ct[x, c] = cot[...]

    w_send(1)
    b_step(2)

    loads[2].wait()
    loads[3].wait()

    def code_rows(i, _):
        rows = pl.ds(pl.multiple_of(i * 64, 64), 64)
        delta = base[rows, :].astype(F32) - loc[rows, :].astype(F32)
        for l in range(2):
            span = slice(l * BLOCK, (l + 1) * BLOCK)
            block = delta[:, span]
            scale = (jnp.max(jnp.abs(block), axis=-1, keepdims=True) + 1e-06).astype(BF).astype(F32)
            code = (block / scale).astype(BF).astype(F32)
            fq[rows, span] = (code * scale).astype(BF)
        return 0

    lax.fori_loop(0, FEAT // 64, code_rows, 0)
    b_step(3)

    def ct_arrive(xs, cc):
        arrive(ct.at[xs, cc], r_ct.at[xs, cc])

    ct_arrive(x, 1 - c)
    pl.when(crossed)(lambda: ct_arrive(x, c))
    for cc in range(2):
        for peer in (xup, xdown):
            send(ct.at[x, cc], ct.at[x, cc], r_ct.at[x, cc], peer)
    b_step(4)
    b_step(5)
    for o in (1, 3, 2):
        rr = ring(r, o)
        send(fq.at[pl.ds(pl.multiple_of(rr * QROWS, QROWS), QROWS)], fr.at[3 - o], r_fr.at[3 - o], (rr, f, t))
    b_step(6)
    b_step(7)

    chain = {}
    for j in range(8):
        for h in range(2):
            chain[j, h] = make(cs.at[j, h], cr.at[j, h], r_cr.at[j, h], (up, down)[h], d != 0)
    final = {}
    for j in range(2, 8):
        for h in range(2):
            q = j % 2
            final[j, h] = make(cs.at[j, h], ng.at[q, h], r_ng.at[q, h], dev(slot(j // 2), c, y, zl), d == 0)

    nt = (((1,), (1,)), ((), ()))
    tn = (((0,), (0,)), ((), ()))

    def a_start(j):
        q, xs = j % 2, slot(j // 2)
        if j < 2:
            arrive_w = pltpu.make_async_copy(wv.at[q], wv.at[q], r_w.at[q])
            arrive_w.wait()
        def part(i, _):
            rows = pl.ds(pl.multiple_of(i * 128, 128), 128)
            ps[j, rows, :] = lax.dot_general(ct[xs, 1 - c, rows, :], wv[q], nt, preferred_element_type=F32).astype(BF)
            return 0
        lax.fori_loop(0, 2, part, 0)
        send(ps.at[j], pr.at[j], r_pr.at[j], sib)
        def mine(i, _):
            rows = pl.ds(pl.multiple_of(i * 128, 128), 128)
            po[j, rows, :] = lax.dot_general(ct[xs, c, rows, :], wv[q], nt, preferred_element_type=F32)
            return 0
        lax.fori_loop(0, 2, mine, 0)

    def a_end(j):
        arrive(pr.at[j], r_pr.at[j])
        for h in range(2):
            rows = pl.ds(h * ROWS, ROWS)
            po[j, rows, :] = po[j, rows, :] + pr[j, rows, :].astype(F32)

            @pl.when(d == (1, 3)[h])
            def _():
                cs[j, h] = po[j, rows, :].astype(BF)
                chain[j, h].start()

    def add(j, h):
        arrive(cr.at[j, h], r_cr.at[j, h])
        return (po[j, pl.ds(h * ROWS, ROWS), :] + cr[j, h].astype(F32)).astype(BF)

    def r_step(s):
        if 0 <= s - 1 < 8:
            j = s - 1

            @pl.when(d == 2)
            def _():
                for h in range(2):
                    cs[j, h] = add(j, h)
                    chain[j, h].start()
        if 0 <= s - 2 < 8:
            i = s - 2
            for h in range(2):
                @pl.when(d == (3, 1)[h])
                def _():
                    cs[i, h] = add(i, h)
                    chain[i, h].start()
        if 0 <= s - 3 < 8:
            k = s - 3

            @pl.when(d == 0)
            def _():
                for h in range(2):
                    if k < 2:
                        ng[k, h] = add(k, h)
                    else:
                        cs[k, h] = add(k, h)
                        final[k, h].start()

    def dw_step(k, q):
        xs = slot(k)
        arrive(pn.at[xs, q, 1 - c], r_pd.at[xs, q])
        right = ct[xs].reshape(2 * TOK, COLS)

        def tile(i, _):
            rows = pl.ds(pl.multiple_of(i * 256, 256), 256)
            left = pn[xs, q, :, :, rows].reshape(2 * TOK, 256)
            part = lax.dot_general(left, right, tn, preferred_element_type=F32)
            if k == 0:
                dw[q, rows, :] = part
            elif k < 3:
                dw[q, rows, :] = dw[q, rows, :] + part
            else:
                dws[q, rows, :] = (dw[q, rows, :] + part).astype(BF)
            return 0

        lax.fori_loop(0, 2, tile, 0)

    a_start(0)
    a_end(0)
    b_step(8)
    r_step(0)
    a_start(1)
    a_end(1)
    b_step(9)
    r_step(1)

    xl, xr = ring(x, 3), ring(x, 1)
    ct_arrive(xl, 0)
    send(ct.at[xl, 0], ct.at[xl, 0], r_ct.at[xl, 0], xup)
    ct_arrive(xr, 1)
    send(ct.at[xr, 1], ct.at[xr, 1], r_ct.at[xr, 1], xdown)
    b_step(10)
    ct_arrive(xr, 0)
    ct_arrive(xl, 1)
    for j in range(2, 6):
        a_start(j)
        a_end(j)
        r_step(j)
        if j >= 4:
            dw_step(0, j - 4)

    for i in range(3):
        arrive(fr.at[i], r_fr.at[i])
    mine = pl.ds(pl.multiple_of(r * QROWS, QROWS), QROWS)

    def code_sum(i, _):
        rows = pl.ds(pl.multiple_of(i * 64, 64), 64)
        own = pl.ds(pl.multiple_of(r * QROWS + i * 64, 64), 64)
        v = fq[own, :].astype(F32)
        for n in range(3):
            v = v + fr[n, rows, :].astype(F32)
        fs[rows, :] = (v * 0.25).astype(BF)
        return 0

    lax.fori_loop(0, QROWS // 64, code_sum, 0)
    keep = pltpu.make_async_copy(fs, fo_hbm.at[mine], lsem.at[4])
    keep.start()
    for o in (1, 3, 2):
        send(fs, fo_hbm.at[mine], r_fo.at[r], (ring(r, o), f, t))

    for k in (1, 2):
        for q in range(2):
            dw_step(k, q)

    far = ring(x, 2)
    ct_arrive(far, 0)
    ct_arrive(far, 1)
    for j in (6, 7):
        a_start(j)
        a_end(j)
        r_step(j)
    w_out = []
    for q in range(2):
        dw_step(3, q)
        rows = pl.ds(q * HALF, HALF)
        send(dws.at[q], dw_hbm.at[rows], r_dw.at[q], swap, crossed)
        w_out.append(pltpu.make_async_copy(dws.at[q], dw_hbm.at[rows], r_dw.at[q]))
        pl.when(straight)(w_out[q].start)
        r_step(8 + q)
    r_step(10)

    def inner_rows(q, i):
        rows = pl.ds(i * 64, 64)
        h, inside = i // 2, pl.ds((i % 2) * 64, 64)
        g = gain[:, q * HALF : (q + 1) * HALF]
        v = ng[q, h, inside, :].astype(F32) * g * res[rows, q * HALF : (q + 1) * HALF].astype(F32)
        if q == 0:
            sq[rows, :] = lanes(v)
        else:
            sq[rows, :] = sq[rows, :] + lanes(v)

    for q in range(2):
        for h in range(2):
            pl.when(d != 0)(lambda q=q, h=h: arrive(ng.at[q, h], r_ng.at[q, h]))
        for i in range(4):
            inner_rows(q, i)
    inns[t] = jnp.broadcast_to(jnp.sum(sq[...].T, axis=0, keepdims=True), (8, TOK))
    for peer in tensors:
        send(inns.at[t], inns.at[t], r_inn.at[t], peer)
    for o in range(1, 8):
        other = lax.rem(t + o, 8)
        arrive(inns.at[other], r_inn.at[other])
    inner = jnp.broadcast_to(jnp.sum(inns[...], axis=0)[0:1] / D, (128, TOK)).T
    rcol[...] = rcol[...] * rcol[...] * inner

    for q in range(2):
        g = gain[:, q * HALF : (q + 1) * HALF]
        for i in range(4):
            rows, h, inside = pl.ds(i * 64, 64), i // 2, pl.ds((i % 2) * 64, 64)
            by = rcol[rows, :]
            for l in range(HALF // 128):
                span = slice(l * 128, (l + 1) * 128)
                full = slice(q * HALF + l * 128, q * HALF + (l + 1) * 128)
                v = ng[q, h, inside, span].astype(F32) * g[:, span] - res[rows, full].astype(F32) * by
                rg_ref[rows, full] = v.astype(BF)

    keep.wait()
    for o in (1, 2, 3):
        rr = ring(r, o)
        arrive(fo_hbm.at[pl.ds(pl.multiple_of(rr * QROWS, QROWS), QROWS)], r_fo.at[rr])
    for q in range(2):
        w_out[q].wait()
    for pred, cp in sends:
        if pred is None:
            cp.wait_send()
        else:
            pl.when(pred)(cp.wait_send)


def local(residual, norm_gain, kv_weight, kv_cotangent, frag_local, frag_base, frag_moment):
    hbm = pl.BlockSpec(memory_space=pl.ANY)
    vmem = pl.BlockSpec(memory_space=pltpu.VMEM)
    dma = pltpu.SemaphoreType.DMA
    residual_grad, weight_grad, outer_grad = pl.pallas_call(
        kernel,
        out_shape=(
            jax.ShapeDtypeStruct((TOK, FEAT), BF),
            jax.ShapeDtypeStruct((FEAT, COLS), BF),
            jax.ShapeDtypeStruct((FEAT, 256), BF),
        ),
        in_specs=[hbm, vmem, hbm, hbm, hbm, hbm],
        out_specs=(vmem, hbm, hbm),
        scratch_shapes=[
            pltpu.VMEM((TOK, FEAT), BF),
            pltpu.VMEM((TOK, COLS), BF),
            pltpu.VMEM((FEAT, 256), BF),
            pltpu.VMEM((FEAT, 256), BF),
            pltpu.VMEM((2, TOK, HALF), BF),
            pltpu.VMEM((4, 2, 2, TOK, HALF), BF),
            pltpu.VMEM((2, HALF, COLS), BF),
            pltpu.VMEM((4, 2, TOK, COLS), BF),
            pltpu.VMEM((8, TOK, HALF), F32),
            pltpu.VMEM((8, TOK, HALF), BF),
            pltpu.VMEM((8, TOK, HALF), BF),
            pltpu.VMEM((8, 2, ROWS, HALF), BF),
            pltpu.VMEM((8, 2, ROWS, HALF), BF),
            pltpu.VMEM((2, 2, ROWS, HALF), BF),
            pltpu.VMEM((2, HALF, COLS), F32),
            pltpu.VMEM((2, HALF, COLS), BF),
            pltpu.VMEM((TOK, 128), F32),
            pltpu.VMEM((TOK, 128), F32),
            pltpu.VMEM((8, 8, TOK), F32),
            pltpu.VMEM((8, 8, TOK), F32),
            pltpu.VMEM((FEAT, 256), BF),
            pltpu.VMEM((3, QROWS, 256), BF),
            pltpu.VMEM((QROWS, 256), BF),
            dma((5,)),
            dma((NSEND,)),
            dma((8,)),
            dma((8,)),
            dma((4, 2, 2)),
            dma((4, 2)),
            dma((2,)),
            dma((4, 2)),
            dma((8,)),
            dma((8, 2)),
            dma((2, 2)),
            dma((2,)),
            dma((3,)),
            dma((4,)),
        ],
        compiler_params=pltpu.CompilerParams(
            collective_id=0, has_side_effects=True, vmem_limit_bytes=52 * 2**20
        ),
        cost_estimate=pl.CostEstimate(flops=6442450944, bytes_accessed=10 * 2**20, transcendentals=0),
    )(residual, norm_gain.reshape(1, FEAT), kv_weight[0], kv_cotangent, frag_local[0], frag_base)
    outer = outer_grad.astype(F32)
    base = frag_base.astype(F32)
    moment_new = 0.9 * frag_moment + outer
    frag_new = (base - 0.7 * (outer + 0.9 * moment_new)).astype(BF)
    return (residual_grad, weight_grad.astype(F32)[None], frag_new, moment_new)


def solution(mesh):
    placed = (
        P(("replica", "fsdp"), "tensor"),
        P("tensor"),
        P("replica", "fsdp", "tensor"),
        P(("replica", "fsdp"), "tensor"),
        P("replica", "fsdp", "tensor"),
        P("fsdp", "tensor"),
        P("fsdp", "tensor"),
    )
    return jax.shard_map(
        local,
        mesh=mesh,
        in_specs=placed,
        out_specs=(
            P(("replica", "fsdp"), "tensor"),
            P("replica", "fsdp", "tensor"),
            P("fsdp", "tensor"),
            P("fsdp", "tensor"),
        ),
        check_vma=False,
    )
```

```python
import jax
import jax.numpy as jnp
from jax import lax
from jax.experimental import pallas as pl
from jax.experimental.pallas import tpu as pltpu
from jax.sharding import PartitionSpec as P

D = 8192
BLOCK = 128
EPS = 1e-05
TOK = 256
FEAT = 1024
COLS = 768
QROWS = 256
F32 = jnp.float32
BF = jnp.bfloat16
MESH = pl.DeviceIdType.MESH
NSEND = 130
LAG = 3


def lanes(v):
    out = v[:, :128]
    for i in range(1, v.shape[1] // 128):
        out = out + v[:, i * 128 : (i + 1) * 128]
    return out


def kernel(
    res_hbm, gain_ref, w_hbm, cot_hbm, loc_hbm, base_hbm,
    rg_ref, dw_hbm, fo_hbm,
    res, cot, loc, base, xg, r1, pn, wv, ct, po, ps, pr, cs, nr, ng, dws,
    sq, rcol, sums, inns, fq, fr, fp, fs,
    lsem, ssem, r_sum, r_inn, r_r1, r_pn, r_pd, r_w, r_ct, r_pr, r_nr, r_dw, r_fr, r_fo,
):
    r = lax.axis_index("replica")
    f = lax.axis_index("fsdp")
    t = lax.axis_index("tensor")
    x, c = lax.div(f, 2), lax.rem(f, 2)
    y, zl = lax.div(t, 2), lax.rem(t, 2)

    def dev(x_, c_, y_, z_, r_=r):
        return (r_, x_ * 2 + c_, y_ * 2 + z_)

    def ring(v, o):
        return lax.rem(v + o, 4)

    sib = dev(x, 1 - c, y, zl)
    swap = dev(x, 1 - c, y, 1 - zl)
    rows_of = [dev(x, c, ring(y, o), zl) for o in range(4)]
    xup, xdown, xfar = (dev(ring(x, o), c, y, zl) for o in (1, 3, 2))
    others = [dev(ring(x, o), c, ring(y, p), zl) for o in (1, 2, 3) for p in (1, 2, 3)]
    tensors = [(r, f, lax.rem(t + o, 8)) for o in range(1, 8)]
    replicas = [(ring(r, o), f, t) for o in (1, 2, 3)]
    d = ring(y - x + 4, 0)
    straight = c == zl
    crossed = c != zl

    barrier = pltpu.get_barrier_semaphore()
    peers = tensors + replicas + others + [sib, swap, xup, xdown, xfar]
    for peer in peers:
        pl.semaphore_signal(barrier, inc=1, device_id=peer, device_id_type=MESH)

    loads = [
        pltpu.make_async_copy(src, dst, lsem.at[i])
        for i, (src, dst) in enumerate(((res_hbm, res), (cot_hbm, cot), (loc_hbm, loc), (base_hbm, base)))
    ]
    for load in loads:
        load.start()

    sends = []

    def make(src, dst, sem, device, pred=None):
        cp = pltpu.make_async_remote_copy(
            src_ref=src, dst_ref=dst, send_sem=ssem.at[len(sends)], recv_sem=sem, device_id=device, device_id_type=MESH
        )
        sends.append((pred, cp))
        return cp

    def send(src, dst, sem, device, pred=None):
        cp = make(src, dst, sem, device, pred)
        if pred is None:
            cp.start()
        else:
            pl.when(pred)(cp.start)

    def arrive(ref, sem):
        pltpu.make_async_remote_copy(
            src_ref=ref, dst_ref=ref, send_sem=ssem.at[0], recv_sem=sem, device_id=sib, device_id_type=MESH
        ).wait_recv()

    gain = jnp.concatenate([gain_ref[i : i + 1, :] for i in range(8)], axis=1).astype(F32)

    loads[0].wait()

    def square_rows(i, _):
        rows = pl.ds(pl.multiple_of(i * 32, 32), 32)
        v = res[rows, :].astype(F32)
        sq[rows, :] = lanes(v * v)
        return 0

    lax.fori_loop(0, TOK // 32, square_rows, 0)
    sums[t] = jnp.broadcast_to(jnp.sum(sq[...].T, axis=0, keepdims=True), (8, TOK))
    loads[1].wait()

    @pl.when(straight)
    def _():
        ct[x, c] = cot[...]

    def slot(k):
        return ring(x, (0, 1, 3, 2)[k])

    def ct_arrive(xs, cc):
        arrive(ct.at[xs, cc], r_ct.at[xs, cc])

    loads[2].wait()
    loads[3].wait()

    def code_rows(i, _):
        rows = pl.ds(pl.multiple_of(i * 64, 64), 64)
        delta = base[rows, :].astype(F32) - loc[rows, :].astype(F32)
        for l in range(2):
            span = slice(l * BLOCK, (l + 1) * BLOCK)
            block = delta[:, span]
            scale = (jnp.max(jnp.abs(block), axis=-1, keepdims=True) + 1e-06).astype(BF).astype(F32)
            code = (block / scale).astype(BF).astype(F32)
            fq[rows, span] = (code * scale).astype(BF)
        return 0

    lax.fori_loop(0, FEAT // 64, code_rows, 0)

    nxt, prv = replicas[0], replicas[2]

    def half_rows(o, h):
        return pl.ds(pl.multiple_of(ring(r, o) * QROWS + h * 128, 128), 128)

    def frag_send():
        send(fq.at[half_rows(2, 0)], fr.at[0], r_fr.at[0], nxt)
        send(fq.at[half_rows(2, 1)], fr.at[1], r_fr.at[1], prv)
        send(fq.at[half_rows(1, 1)], fr.at[2], r_fr.at[2], nxt)
        send(fq.at[half_rows(3, 0)], fr.at[3], r_fr.at[3], prv)

    pl.semaphore_wait(barrier, len(peers))

    for peer in tensors:
        send(sums.at[t], sums.at[t], r_sum.at[t], peer)

    send(cot, ct.at[x, c], r_ct.at[x, c], dev(x, zl, y, 1 - zl))
    send(cot, ct.at[x, c], r_ct.at[x, c], sib, crossed)
    over = []
    for cc in (c, 1 - c):
        ref = ct.at[x, cc]
        over.append([make(ref, ref, r_ct.at[x, cc], peer) for peer in (xup, xdown)])

    @pl.when(straight)
    def _():
        for cp in over[0]:
            cp.start()

    w_own = [pltpu.make_async_copy(w_hbm.at[pl.ds(q * 256, 256)], wv.at[q], r_w.at[q]) for q in range(4)]

    @pl.when(straight)
    def _():
        for q in range(4):
            w_own[q].start()

    for q in range(4):
        send(w_hbm.at[pl.ds(q * 256, 256)], wv.at[q], r_w.at[q], swap, crossed)

    @pl.when(straight)
    def _():
        ct_arrive(x, 1 - c)
        for cp in over[1]:
            cp.start()

    frag_send()

    for o in range(1, 8):
        other = lax.rem(t + o, 8)
        arrive(sums.at[other], r_sum.at[other])
    total = jnp.sum(sums[...], axis=0)[0:1]
    rinv = lax.rsqrt(total / D + EPS)
    rcol[...] = jnp.broadcast_to(rinv, (128, TOK)).T

    def scale_rows(i, _):
        rows = pl.ds(pl.multiple_of(i * 32, 32), 32)
        by = rcol[rows, :]
        for l in range(FEAT // 128):
            span = slice(l * 128, (l + 1) * 128)
            inside = slice(l % 2 * 128, (l % 2 + 1) * 128)
            xg[l // 2, rows, inside] = (res[rows, span].astype(F32) * by * gain[:, span]).astype(BF)
        return 0

    lax.fori_loop(0, TOK // 32, scale_rows, 0)

    r1[0] = xg[0]
    for m in (1, 3, 2):
        send(xg.at[m], r1.at[m], r_r1.at[m], rows_of[m])

    xl, xr = ring(x, 3), ring(x, 1)
    hand = [
        make(ct.at[xl, 0], ct.at[xl, 0], r_ct.at[xl, 0], xup),
        make(ct.at[xr, 1], ct.at[xr, 1], r_ct.at[xr, 1], xdown),
    ]

    def hand_on():
        ct_arrive(xl, 0)
        hand[0].start()
        ct_arrive(xr, 1)
        hand[1].start()

    def columns():
        for m in (1, 3, 2):
            arrive(r1.at[m], r_r1.at[m])
        for o in (1, 3, 2):
            m = ring(d, 4 - o)
            send(r1.at[m], pn.at[m, x, c], r_pn.at[m, x], dev(ring(x, o), c, y, zl))
        pn[d, x, c] = r1[d]

    def spread(k):
        xs = slot(k)
        ref = pn.at[d, xs, c]
        if k:
            arrive(ref, r_pn.at[d, xs])
        for o in (1, 3, 2):
            send(ref, ref, r_pn.at[d, xs], rows_of[o])

    def quarter(i):
        return ring(d, (0, 1, 3, 2)[i])

    def pair(i):
        m = quarter(i)
        if i:
            for k in range(4):
                arrive(pn.at[m, slot(k), c], r_pn.at[m, slot(k)])
        send(pn.at[m, :, c], pn.at[m, :, c], r_pd.at[m], sib)

    nt = (((1,), (1,)), ((), ()))
    tn = (((0,), (0,)), ((), ()))

    def offset(j):
        q, p = j // 4, j % 4
        if q:
            return ring(y, p)
        if p == 3:
            return 2
        o = lax.rem(y + p, 3)
        return o + lax.div(o, 2)

    def a_start(j):
        q, xs = j // 4, ring(x, offset(j))
        right = wv[q]
        ps[j] = lax.dot_general(ct[xs, 1 - c], right, nt, preferred_element_type=F32).astype(BF)
        send(ps.at[j], pr.at[j], r_pr.at[j], sib)
        po[j % 4] = lax.dot_general(ct[xs, c], right, nt, preferred_element_type=F32)

    def a_end(j):
        q, o = j // 4, offset(j)
        arrive(pr.at[j], r_pr.at[j])
        total = (po[j % 4] + pr[j].astype(F32)).astype(BF)
        cs[j] = total
        send(cs.at[j], nr.at[y, q], r_nr.at[y, q], dev(ring(x, o), c, x, zl), d + o != 0)

        @pl.when(d + o == 0)
        def _():
            nr[y, q] = total

    w_out = []

    def dw_step(i):
        m = quarter(i)
        arrive(pn.at[m, :, 1 - c], r_pd.at[m])
        left = pn[m].reshape(8 * TOK, 256)
        right = ct[...].reshape(8 * TOK, COLS)
        dws[m] = lax.dot_general(left, right, tn, preferred_element_type=F32).astype(BF)
        rows = pl.ds(pl.multiple_of(m * 256, 256), 256)
        send(dws.at[m], dw_hbm.at[rows], r_dw.at[m], swap, crossed)
        w_out.append(pltpu.make_async_copy(dws.at[m], dw_hbm.at[rows], r_dw.at[m]))
        pl.when(straight)(w_out[i].start)

    mine = pl.ds(pl.multiple_of(r * QROWS, QROWS), QROWS)
    keep = pltpu.make_async_copy(fs, fo_hbm.at[mine], lsem.at[4])

    def frag_pass():
        for h, o, peer in ((0, 1, nxt), (1, 3, prv)):
            arrive(fr.at[h], r_fr.at[h])
            fp[h] = (fr[h].astype(F32) + fq[half_rows(o, h), :].astype(F32)).astype(BF)
            send(fp.at[h], fr.at[4 + h], r_fr.at[4 + h], peer)

    def frag_sum():
        for h in range(2):
            arrive(fr.at[4 + h], r_fr.at[4 + h])
            arrive(fr.at[3 - h], r_fr.at[3 - h])
            v = fq[half_rows(0, h), :].astype(F32) + fr[4 + h].astype(F32) + fr[3 - h].astype(F32)
            fs[pl.ds(h * 128, 128), :] = (v * 0.25).astype(BF)
        keep.start()
        for h in range(2):
            span = pl.ds(h * 128, 128)
            for peer in (nxt, prv):
                send(fs.at[span], fo_hbm.at[half_rows(0, h)], r_fo.at[r, h], peer)

    def frag_forward():
        for h, o, peer in ((0, 3, nxt), (1, 1, prv)):
            ref, sem = fo_hbm.at[half_rows(o, h)], r_fo.at[ring(r, o), h]
            arrive(ref, sem)
            send(ref, ref, sem, peer)

    def w_arrive(q):
        pltpu.make_async_copy(wv.at[q], wv.at[q], r_w.at[q]).wait()

    columns()
    spread(0)

    @pl.when(crossed)
    def _():
        for cc, cps in zip((c, 1 - c), over):
            ct_arrive(x, cc)
            for cp in cps:
                cp.start()

    pl.when(straight)(hand_on)
    for k in (1, 2, 3):
        spread(k)
    pair(0)
    pl.when(crossed)(hand_on)
    ct_arrive(xr, 0)
    ct_arrive(xl, 1)
    for j in range(16):
        if j == 3:
            ct_arrive(ring(x, 2), 0)
            ct_arrive(ring(x, 2), 1)
        if j % 4 == 0:
            w_arrive(j // 4)
        a_start(j)
        if j == 7:
            dw_step(0)
        if j >= LAG:
            a_end(j - LAG)
        if j == 11:
            frag_pass()
    for j in range(16 - LAG, 16):
        a_end(j)
    pair(1)
    pair(2)
    dw_step(1)
    frag_sum()
    pair(3)
    dw_step(2)
    frag_forward()
    dw_step(3)

    for q in range(4):
        span = slice(q * 256, (q + 1) * 256)
        for p in range(4):
            if p == 0:
                pl.when(d != 0)(lambda q=q: arrive(nr.at[y, q], r_nr.at[y, q]))
            else:
                arrive(nr.at[ring(y, p), q], r_nr.at[ring(y, p), q])

        def inner_rows(i, _):
            rows = pl.ds(pl.multiple_of(i * 32, 32), 32)
            v = nr[0, q, rows, :].astype(F32)
            for p in range(1, 4):
                v = v + nr[p, q, rows, :].astype(F32)
            v = v * gain[:, span]
            ng[rows, span] = v
            v = lanes(v * res[rows, span].astype(F32))
            sq[rows, :] = v if q == 0 else sq[rows, :] + v
            return 0

        lax.fori_loop(0, TOK // 32, inner_rows, 0)
    inns[t] = jnp.broadcast_to(jnp.sum(sq[...].T, axis=0, keepdims=True), (8, TOK))
    for peer in tensors:
        send(inns.at[t], inns.at[t], r_inn.at[t], peer)
    for o in range(1, 8):
        other = lax.rem(t + o, 8)
        arrive(inns.at[other], r_inn.at[other])
    inner = jnp.broadcast_to(jnp.sum(inns[...], axis=0)[0:1] / D, (128, TOK)).T
    sq[...] = rcol[...] * rcol[...] * rcol[...] * inner

    def out_rows(i, _):
        rows = pl.ds(pl.multiple_of(i * 32, 32), 32)
        by, rv = sq[rows, :], rcol[rows, :]
        for l in range(FEAT // 128):
            span = slice(l * 128, (l + 1) * 128)
            rg_ref[rows, span] = (ng[rows, span] * rv - res[rows, span].astype(F32) * by).astype(BF)
        return 0

    lax.fori_loop(0, TOK // 32, out_rows, 0)

    keep.wait()
    for o, h in ((3, 1), (1, 0), (2, 0), (2, 1)):
        arrive(fo_hbm.at[half_rows(o, h)], r_fo.at[ring(r, o), h])
    for i in range(4):
        w_out[i].wait()
    for pred, cp in sends:
        if pred is None:
            cp.wait_send()
        else:
            pl.when(pred)(cp.wait_send)


def finish(dw_ref, outer_ref, base_ref, moment_ref, rg_in, dw_out, frag_out, moment_out, rg_out):
    dw_out[...] = dw_ref[...].astype(F32)
    outer = outer_ref[...].astype(F32)
    moment = 0.9 * moment_ref[...] + outer
    moment_out[...] = moment
    frag_out[...] = (base_ref[...].astype(F32) - 0.7 * (outer + 0.9 * moment)).astype(BF)
    rg_out[...] = rg_in[...]


def local(residual, norm_gain, kv_weight, kv_cotangent, frag_local, frag_base, frag_moment):
    hbm = pl.BlockSpec(memory_space=pl.ANY)
    vmem = pl.BlockSpec(memory_space=pltpu.VMEM)
    dma = pltpu.SemaphoreType.DMA
    residual_grad, weight_grad, outer_grad = pl.pallas_call(
        kernel,
        out_shape=(
            jax.ShapeDtypeStruct((TOK, FEAT), BF),
            jax.ShapeDtypeStruct((FEAT, COLS), BF),
            jax.ShapeDtypeStruct((FEAT, 256), BF),
        ),
        in_specs=[hbm, vmem, hbm, hbm, hbm, hbm],
        out_specs=(vmem, hbm, hbm),
        scratch_shapes=[
            pltpu.VMEM((TOK, FEAT), BF),
            pltpu.VMEM((TOK, COLS), BF),
            pltpu.VMEM((FEAT, 256), BF),
            pltpu.VMEM((FEAT, 256), BF),
            pltpu.VMEM((4, TOK, 256), BF),
            pltpu.VMEM((4, TOK, 256), BF),
            pltpu.VMEM((4, 4, 2, TOK, 256), BF),
            pltpu.VMEM((4, 256, COLS), BF),
            pltpu.VMEM((4, 2, TOK, COLS), BF),
            pltpu.VMEM((4, TOK, 256), F32),
            pltpu.VMEM((16, TOK, 256), BF),
            pltpu.VMEM((16, TOK, 256), BF),
            pltpu.VMEM((16, TOK, 256), BF),
            pltpu.VMEM((4, 4, TOK, 256), BF),
            pltpu.VMEM((TOK, FEAT), F32),
            pltpu.VMEM((4, 256, COLS), BF),
            pltpu.VMEM((TOK, 128), F32),
            pltpu.VMEM((TOK, 128), F32),
            pltpu.VMEM((8, 8, TOK), F32),
            pltpu.VMEM((8, 8, TOK), F32),
            pltpu.VMEM((FEAT, 256), BF),
            pltpu.VMEM((6, 128, 256), BF),
            pltpu.VMEM((2, 128, 256), BF),
            pltpu.VMEM((QROWS, 256), BF),
            dma((5,)),
            dma((NSEND,)),
            dma((8,)),
            dma((8,)),
            dma((4,)),
            dma((4, 4)),
            dma((4,)),
            dma((4,)),
            dma((4, 2)),
            dma((16,)),
            dma((4, 4)),
            dma((4,)),
            dma((6,)),
            dma((4, 2)),
        ],
        compiler_params=pltpu.CompilerParams(
            collective_id=0, has_side_effects=True, vmem_limit_bytes=60 * 2**20
        ),
        cost_estimate=pl.CostEstimate(flops=6442450944, bytes_accessed=10 * 2**20, transcendentals=0),
    )(residual, norm_gain.reshape(8, 128), kv_weight[0], kv_cotangent, frag_local[0], frag_base)
    def rows(n, width):
        return pl.BlockSpec((n, width), lambda i: (i, 0))

    steps = 4
    specs = [rows(FEAT // steps, w) for w in (COLS, 256, 256, 256)] + [rows(TOK // steps, FEAT)]
    weight_grad, frag_new, moment_new, residual_grad = pl.pallas_call(
        finish,
        grid=(steps,),
        out_shape=(
            jax.ShapeDtypeStruct((FEAT, COLS), F32),
            jax.ShapeDtypeStruct((FEAT, 256), BF),
            jax.ShapeDtypeStruct((FEAT, 256), F32),
            jax.ShapeDtypeStruct((TOK, FEAT), BF),
        ),
        in_specs=specs,
        out_specs=(specs[0], specs[1], specs[1], specs[4]),
    )(weight_grad, outer_grad, frag_base, frag_moment, residual_grad)
    return (residual_grad, weight_grad[None], frag_new, moment_new)


def solution(mesh):
    placed = (
        P(("replica", "fsdp"), "tensor"),
        P("tensor"),
        P("replica", "fsdp", "tensor"),
        P(("replica", "fsdp"), "tensor"),
        P("replica", "fsdp", "tensor"),
        P("fsdp", "tensor"),
        P("fsdp", "tensor"),
    )
    return jax.shard_map(
        local,
        mesh=mesh,
        in_specs=placed,
        out_specs=(
            P(("replica", "fsdp"), "tensor"),
            P("replica", "fsdp", "tensor"),
            P("fsdp", "tensor"),
            P("fsdp", "tensor"),
        ),
        check_vma=False,
    )
```

```python
import jax
import jax.numpy as jnp
from jax import lax
from jax.experimental import pallas as pl
from jax.experimental.pallas import tpu as pltpu
from jax.sharding import PartitionSpec as P

D = 8192
BLOCK = 128
EPS = 1e-05
TOK = 256
FEAT = 1024
COLS = 768
QROWS = 256
F32 = jnp.float32
BF = jnp.bfloat16
MESH = pl.DeviceIdType.MESH
NSEND = 130
LAG = 3


def lanes(v):
    out = v[:, :128]
    for i in range(1, v.shape[1] // 128):
        out = out + v[:, i * 128 : (i + 1) * 128]
    return out


def kernel(
    res_hbm, gain_ref, w_hbm, cot_hbm, loc_hbm, base_hbm,
    rg_ref, dw_hbm, fo_hbm,
    res, cot, loc, base, xg, r1, pn, wv, ct, po, ps, pr, cs, nr, ng, dws,
    sq, rcol, sums, inns, fq, fr, fp, fs,
    lsem, ssem, r_sum, r_inn, r_r1, r_pn, r_pd, r_w, r_ct, r_pr, r_nr, r_dw, r_fr, r_fo,
):
    r = lax.axis_index("replica")
    f = lax.axis_index("fsdp")
    t = lax.axis_index("tensor")
    x, c = lax.div(f, 2), lax.rem(f, 2)
    y, zl = lax.div(t, 2), lax.rem(t, 2)

    def dev(x_, c_, y_, z_, r_=r):
        return (r_, x_ * 2 + c_, y_ * 2 + z_)

    def ring(v, o):
        return lax.rem(v + o, 4)

    sib = dev(x, 1 - c, y, zl)
    swap = dev(x, 1 - c, y, 1 - zl)
    rows_of = [dev(x, c, ring(y, o), zl) for o in range(4)]
    xup, xdown, xfar = (dev(ring(x, o), c, y, zl) for o in (1, 3, 2))
    others = [dev(ring(x, o), c, ring(y, p), zl) for o in (1, 2, 3) for p in (1, 2, 3)]
    tensors = [(r, f, lax.rem(t + o, 8)) for o in range(1, 8)]
    replicas = [(ring(r, o), f, t) for o in (1, 2, 3)]
    d = ring(y - x + 4, 0)
    straight = c == zl
    crossed = c != zl

    barrier = pltpu.get_barrier_semaphore()
    peers = tensors + replicas + others + [sib, swap, xup, xdown, xfar]
    for peer in peers:
        pl.semaphore_signal(barrier, inc=1, device_id=peer, device_id_type=MESH)

    loads = [
        pltpu.make_async_copy(src, dst, lsem.at[i])
        for i, (src, dst) in enumerate(((res_hbm, res), (cot_hbm, cot), (loc_hbm, loc), (base_hbm, base)))
    ]
    for load in loads:
        load.start()

    sends = []

    def make(src, dst, sem, device, pred=None):
        cp = pltpu.make_async_remote_copy(
            src_ref=src, dst_ref=dst, send_sem=ssem.at[len(sends)], recv_sem=sem, device_id=device, device_id_type=MESH
        )
        sends.append((pred, cp))
        return cp

    def send(src, dst, sem, device, pred=None):
        cp = make(src, dst, sem, device, pred)
        if pred is None:
            cp.start()
        else:
            pl.when(pred)(cp.start)

    def arrive(ref, sem):
        pltpu.make_async_remote_copy(
            src_ref=ref, dst_ref=ref, send_sem=ssem.at[0], recv_sem=sem, device_id=sib, device_id_type=MESH
        ).wait_recv()

    gain = jnp.concatenate([gain_ref[i : i + 1, :] for i in range(8)], axis=1).astype(F32)

    loads[0].wait()

    def square_rows(i, _):
        rows = pl.ds(pl.multiple_of(i * 32, 32), 32)
        v = res[rows, :].astype(F32)
        sq[rows, :] = lanes(v * v)
        g = (v * gain).astype(BF)
        for m in range(4):
            xg[m, rows, :] = g[:, m * 256 : (m + 1) * 256]
        return 0

    lax.fori_loop(0, TOK // 32, square_rows, 0)
    r1[0] = xg[0]
    sums[t] = jnp.broadcast_to(jnp.sum(sq[...].T, axis=0, keepdims=True), (8, TOK))
    loads[1].wait()

    @pl.when(straight)
    def _():
        ct[x, c] = cot[...]

    def slot(k):
        return ring(x, (0, 1, 3, 2)[k])

    def ct_arrive(xs, cc):
        arrive(ct.at[xs, cc], r_ct.at[xs, cc])

    loads[2].wait()
    loads[3].wait()

    def code_rows(i, _):
        rows = pl.ds(pl.multiple_of(i * 64, 64), 64)
        delta = base[rows, :].astype(F32) - loc[rows, :].astype(F32)
        for l in range(2):
            span = slice(l * BLOCK, (l + 1) * BLOCK)
            block = delta[:, span]
            scale = (jnp.max(jnp.abs(block), axis=-1, keepdims=True) + 1e-06).astype(BF).astype(F32)
            code = (block / scale).astype(BF).astype(F32)
            fq[rows, span] = (code * scale).astype(BF)
        return 0

    lax.fori_loop(0, FEAT // 64, code_rows, 0)

    nxt, prv = replicas[0], replicas[2]

    def half_rows(o, h):
        return pl.ds(pl.multiple_of(ring(r, o) * QROWS + h * 128, 128), 128)

    def frag_send():
        send(fq.at[half_rows(2, 0)], fr.at[0], r_fr.at[0], nxt)
        send(fq.at[half_rows(2, 1)], fr.at[1], r_fr.at[1], prv)
        send(fq.at[half_rows(1, 1)], fr.at[2], r_fr.at[2], nxt)
        send(fq.at[half_rows(3, 0)], fr.at[3], r_fr.at[3], prv)

    pl.semaphore_wait(barrier, len(peers))

    for peer in tensors:
        send(sums.at[t], sums.at[t], r_sum.at[t], peer)

    for m in (1, 3, 2):
        send(xg.at[m], r1.at[m], r_r1.at[m], rows_of[m])

    send(cot, ct.at[x, c], r_ct.at[x, c], dev(x, zl, y, 1 - zl))
    send(cot, ct.at[x, c], r_ct.at[x, c], sib, crossed)
    over = []
    for cc in (c, 1 - c):
        ref = ct.at[x, cc]
        over.append([make(ref, ref, r_ct.at[x, cc], peer) for peer in (xup, xdown)])

    @pl.when(straight)
    def _():
        for cp in over[0]:
            cp.start()

    w_own = [pltpu.make_async_copy(w_hbm.at[pl.ds(q * 256, 256)], wv.at[q], r_w.at[q]) for q in range(4)]

    @pl.when(straight)
    def _():
        for q in range(4):
            w_own[q].start()

    for q in range(4):
        send(w_hbm.at[pl.ds(q * 256, 256)], wv.at[q], r_w.at[q], swap, crossed)

    @pl.when(straight)
    def _():
        ct_arrive(x, 1 - c)
        for cp in over[1]:
            cp.start()

    for o in range(1, 8):
        other = lax.rem(t + o, 8)
        arrive(sums.at[other], r_sum.at[other])
    total = jnp.sum(sums[...], axis=0)[0:1]
    rinv = lax.rsqrt(total / D + EPS)
    rcol[...] = jnp.broadcast_to(rinv, (128, TOK)).T

    xl, xr = ring(x, 3), ring(x, 1)
    hand = [
        make(ct.at[xl, 0], ct.at[xl, 0], r_ct.at[xl, 0], xup),
        make(ct.at[xr, 1], ct.at[xr, 1], r_ct.at[xr, 1], xdown),
    ]

    def hand_on():
        ct_arrive(xl, 0)
        hand[0].start()
        ct_arrive(xr, 1)
        hand[1].start()

    def times_rinv(m):
        by = rcol[...]
        return jnp.concatenate([(r1[m, :, l * 128 : (l + 1) * 128].astype(F32) * by).astype(BF) for l in range(2)], axis=1)

    def columns():
        for m in (1, 3, 2):
            arrive(r1.at[m], r_r1.at[m])
        for o in (1, 3, 2):
            m = ring(d, 4 - o)
            r1[m] = times_rinv(m)
            send(r1.at[m], pn.at[m, x, c], r_pn.at[m, x], dev(ring(x, o), c, y, zl))
        pn[d, x, c] = times_rinv(d)

    def spread(k):
        xs = slot(k)
        ref = pn.at[d, xs, c]
        if k:
            arrive(ref, r_pn.at[d, xs])
        for o in (1, 3, 2):
            send(ref, ref, r_pn.at[d, xs], rows_of[o])

    def quarter(i):
        return ring(d, (0, 1, 3, 2)[i])

    def pair(i):
        m = quarter(i)
        if i:
            for k in range(4):
                arrive(pn.at[m, slot(k), c], r_pn.at[m, slot(k)])
        send(pn.at[m, :, c], pn.at[m, :, c], r_pd.at[m], sib)

    nt = (((1,), (1,)), ((), ()))
    tn = (((0,), (0,)), ((), ()))

    plan = [(0, 0), (0, 1), (0, 2), (1, 0), (1, 1), (1, 2), (0, 3)]
    plan += [(2, 4 + p) for p in range(4)] + [(1, 3)] + [(3, 4 + p) for p in range(4)]

    def offset(j):
        p = plan[j][1]
        if p > 3:
            return ring(y, p - 4)
        if p == 3:
            return 2
        o = lax.rem(y + p, 3)
        return o + lax.div(o, 2)

    def a_start(j):
        q, xs = plan[j][0], ring(x, offset(j))
        right = wv[q]
        ps[j] = lax.dot_general(ct[xs, 1 - c], right, nt, preferred_element_type=F32).astype(BF)
        send(ps.at[j], pr.at[j], r_pr.at[j], sib)
        po[j % 4] = lax.dot_general(ct[xs, c], right, nt, preferred_element_type=F32)

    def a_end(j):
        q, o = plan[j][0], offset(j)
        arrive(pr.at[j], r_pr.at[j])
        total = (po[j % 4] + pr[j].astype(F32)).astype(BF)
        cs[j] = total
        send(cs.at[j], nr.at[y, q], r_nr.at[y, q], dev(ring(x, o), c, x, zl), d + o != 0)

        @pl.when(d + o == 0)
        def _():
            nr[y, q] = total

    w_out = []

    def dw_step(i):
        m = quarter(i)
        arrive(pn.at[m, :, 1 - c], r_pd.at[m])
        left = pn[m].reshape(8 * TOK, 256)
        right = ct[...].reshape(8 * TOK, COLS)
        dws[m] = lax.dot_general(left, right, tn, preferred_element_type=F32).astype(BF)
        rows = pl.ds(pl.multiple_of(m * 256, 256), 256)
        send(dws.at[m], dw_hbm.at[rows], r_dw.at[m], swap, crossed)
        w_out.append(pltpu.make_async_copy(dws.at[m], dw_hbm.at[rows], r_dw.at[m]))
        pl.when(straight)(w_out[i].start)

    mine = pl.ds(pl.multiple_of(r * QROWS, QROWS), QROWS)
    keep = pltpu.make_async_copy(fs, fo_hbm.at[mine], lsem.at[4])

    def frag_pass():
        for h, o, peer in ((0, 1, nxt), (1, 3, prv)):
            arrive(fr.at[h], r_fr.at[h])
            fp[h] = (fr[h].astype(F32) + fq[half_rows(o, h), :].astype(F32)).astype(BF)
            send(fp.at[h], fr.at[4 + h], r_fr.at[4 + h], peer)

    def frag_sum():
        for h in range(2):
            arrive(fr.at[4 + h], r_fr.at[4 + h])
            arrive(fr.at[3 - h], r_fr.at[3 - h])
            v = fq[half_rows(0, h), :].astype(F32) + fr[4 + h].astype(F32) + fr[3 - h].astype(F32)
            fs[pl.ds(h * 128, 128), :] = (v * 0.25).astype(BF)
        keep.start()
        for h in range(2):
            span = pl.ds(h * 128, 128)
            for peer in (nxt, prv):
                send(fs.at[span], fo_hbm.at[half_rows(0, h)], r_fo.at[r, h], peer)

    def frag_forward():
        for h, o, peer in ((0, 3, nxt), (1, 1, prv)):
            ref, sem = fo_hbm.at[half_rows(o, h)], r_fo.at[ring(r, o), h]
            arrive(ref, sem)
            send(ref, ref, sem, peer)

    def w_arrive(q):
        pltpu.make_async_copy(wv.at[q], wv.at[q], r_w.at[q]).wait()

    columns()
    spread(0)
    frag_send()

    @pl.when(crossed)
    def _():
        for cc, cps in zip((c, 1 - c), over):
            ct_arrive(x, cc)
            for cp in cps:
                cp.start()

    pl.when(straight)(hand_on)
    for k in (1, 2, 3):
        spread(k)
    pair(0)
    pl.when(crossed)(hand_on)
    ct_arrive(xr, 0)
    ct_arrive(xl, 1)
    for j in range(16):
        if plan[j] == (0, 3):
            ct_arrive(ring(x, 2), 0)
            ct_arrive(ring(x, 2), 1)
        if j in (0, 3, 7, 12):
            w_arrive(plan[j][0])
        a_start(j)
        if j == 9:
            dw_step(0)
        if j >= LAG:
            a_end(j - LAG)
        if j == 11:
            frag_pass()
        if j == 10:
            pair(1)
        if j == 13:
            dw_step(1)
    for j in range(16 - LAG, 16):
        a_end(j)
    pair(2)
    frag_sum()
    pair(3)
    dw_step(2)
    frag_forward()
    dw_step(3)

    for q in range(4):
        span = slice(q * 256, (q + 1) * 256)
        for p in range(4):
            if p == 0:
                pl.when(d != 0)(lambda q=q: arrive(nr.at[y, q], r_nr.at[y, q]))
            else:
                arrive(nr.at[ring(y, p), q], r_nr.at[ring(y, p), q])

        def inner_rows(i, _):
            rows = pl.ds(pl.multiple_of(i * 32, 32), 32)
            v = nr[0, q, rows, :].astype(F32)
            for p in range(1, 4):
                v = v + nr[p, q, rows, :].astype(F32)
            v = v * gain[:, span]
            ng[rows, span] = v
            v = lanes(v * res[rows, span].astype(F32))
            sq[rows, :] = v if q == 0 else sq[rows, :] + v
            return 0

        lax.fori_loop(0, TOK // 32, inner_rows, 0)
    inns[t] = jnp.broadcast_to(jnp.sum(sq[...].T, axis=0, keepdims=True), (8, TOK))
    for peer in tensors:
        send(inns.at[t], inns.at[t], r_inn.at[t], peer)
    for o in range(1, 8):
        other = lax.rem(t + o, 8)
        arrive(inns.at[other], r_inn.at[other])
    inner = jnp.broadcast_to(jnp.sum(inns[...], axis=0)[0:1] / D, (128, TOK)).T
    sq[...] = rcol[...] * rcol[...] * rcol[...] * inner

    def out_rows(i, _):
        rows = pl.ds(pl.multiple_of(i * 32, 32), 32)
        by, rv = sq[rows, :], rcol[rows, :]
        for l in range(FEAT // 128):
            span = slice(l * 128, (l + 1) * 128)
            rg_ref[rows, span] = (ng[rows, span] * rv - res[rows, span].astype(F32) * by).astype(BF)
        return 0

    lax.fori_loop(0, TOK // 32, out_rows, 0)

    keep.wait()
    for o, h in ((3, 1), (1, 0), (2, 0), (2, 1)):
        arrive(fo_hbm.at[half_rows(o, h)], r_fo.at[ring(r, o), h])
    for i in range(4):
        w_out[i].wait()
    for pred, cp in sends:
        if pred is None:
            cp.wait_send()
        else:
            pl.when(pred)(cp.wait_send)


def finish(dw_ref, outer_ref, base_ref, moment_ref, rg_in, dw_out, frag_out, moment_out, rg_out):
    dw_out[...] = dw_ref[...].astype(F32)
    outer = outer_ref[...].astype(F32)
    moment = 0.9 * moment_ref[...] + outer
    moment_out[...] = moment
    frag_out[...] = (base_ref[...].astype(F32) - 0.7 * (outer + 0.9 * moment)).astype(BF)
    rg_out[...] = rg_in[...]


def local(residual, norm_gain, kv_weight, kv_cotangent, frag_local, frag_base, frag_moment):
    hbm = pl.BlockSpec(memory_space=pl.ANY)
    vmem = pl.BlockSpec(memory_space=pltpu.VMEM)
    dma = pltpu.SemaphoreType.DMA
    residual_grad, weight_grad, outer_grad = pl.pallas_call(
        kernel,
        out_shape=(
            jax.ShapeDtypeStruct((TOK, FEAT), BF),
            jax.ShapeDtypeStruct((FEAT, COLS), BF),
            jax.ShapeDtypeStruct((FEAT, 256), BF),
        ),
        in_specs=[hbm, vmem, hbm, hbm, hbm, hbm],
        out_specs=(vmem, hbm, hbm),
        scratch_shapes=[
            pltpu.VMEM((TOK, FEAT), BF),
            pltpu.VMEM((TOK, COLS), BF),
            pltpu.VMEM((FEAT, 256), BF),
            pltpu.VMEM((FEAT, 256), BF),
            pltpu.VMEM((4, TOK, 256), BF),
            pltpu.VMEM((4, TOK, 256), BF),
            pltpu.VMEM((4, 4, 2, TOK, 256), BF),
            pltpu.VMEM((4, 256, COLS), BF),
            pltpu.VMEM((4, 2, TOK, COLS), BF),
            pltpu.VMEM((4, TOK, 256), F32),
            pltpu.VMEM((16, TOK, 256), BF),
            pltpu.VMEM((16, TOK, 256), BF),
            pltpu.VMEM((16, TOK, 256), BF),
            pltpu.VMEM((4, 4, TOK, 256), BF),
            pltpu.VMEM((TOK, FEAT), F32),
            pltpu.VMEM((4, 256, COLS), BF),
            pltpu.VMEM((TOK, 128), F32),
            pltpu.VMEM((TOK, 128), F32),
            pltpu.VMEM((8, 8, TOK), F32),
            pltpu.VMEM((8, 8, TOK), F32),
            pltpu.VMEM((FEAT, 256), BF),
            pltpu.VMEM((6, 128, 256), BF),
            pltpu.VMEM((2, 128, 256), BF),
            pltpu.VMEM((QROWS, 256), BF),
            dma((5,)),
            dma((NSEND,)),
            dma((8,)),
            dma((8,)),
            dma((4,)),
            dma((4, 4)),
            dma((4,)),
            dma((4,)),
            dma((4, 2)),
            dma((16,)),
            dma((4, 4)),
            dma((4,)),
            dma((6,)),
            dma((4, 2)),
        ],
        compiler_params=pltpu.CompilerParams(
            collective_id=0, has_side_effects=True, vmem_limit_bytes=60 * 2**20
        ),
        cost_estimate=pl.CostEstimate(flops=6442450944, bytes_accessed=10 * 2**20, transcendentals=0),
    )(residual, norm_gain.reshape(8, 128), kv_weight[0], kv_cotangent, frag_local[0], frag_base)
    def rows(n, width):
        return pl.BlockSpec((n, width), lambda i: (i, 0))

    steps = 2
    specs = [rows(FEAT // steps, w) for w in (COLS, 256, 256, 256)] + [rows(TOK // steps, FEAT)]
    weight_grad, frag_new, moment_new, residual_grad = pl.pallas_call(
        finish,
        grid=(steps,),
        out_shape=(
            jax.ShapeDtypeStruct((FEAT, COLS), F32),
            jax.ShapeDtypeStruct((FEAT, 256), BF),
            jax.ShapeDtypeStruct((FEAT, 256), F32),
            jax.ShapeDtypeStruct((TOK, FEAT), BF),
        ),
        in_specs=specs,
        out_specs=(specs[0], specs[1], specs[1], specs[4]),
    )(weight_grad, outer_grad, frag_base, frag_moment, residual_grad)
    return (residual_grad, weight_grad[None], frag_new, moment_new)


def solution(mesh):
    placed = (
        P(("replica", "fsdp"), "tensor"),
        P("tensor"),
        P("replica", "fsdp", "tensor"),
        P(("replica", "fsdp"), "tensor"),
        P("replica", "fsdp", "tensor"),
        P("fsdp", "tensor"),
        P("fsdp", "tensor"),
    )
    return jax.shard_map(
        local,
        mesh=mesh,
        in_specs=placed,
        out_specs=(
            P(("replica", "fsdp"), "tensor"),
            P("replica", "fsdp", "tensor"),
            P("fsdp", "tensor"),
            P("fsdp", "tensor"),
        ),
        check_vma=False,
    )
```

```python
import jax
import jax.numpy as jnp
from jax import lax
from jax.experimental import pallas as pl
from jax.experimental.pallas import tpu as pltpu
from jax.sharding import PartitionSpec as P

D = 8192
BLOCK = 128
EPS = 1e-05
TOK = 256
FEAT = 1024
COLS = 768
QROWS = 256
F32 = jnp.float32
BF = jnp.bfloat16
MESH = pl.DeviceIdType.MESH
NSEND = 130
LAG = 3


def lanes(v):
    out = v[:, :128]
    for i in range(1, v.shape[1] // 128):
        out = out + v[:, i * 128 : (i + 1) * 128]
    return out


def kernel(
    res_hbm, gain_ref, w_hbm, cot_hbm, loc_hbm, base_hbm,
    rg_ref, dw_hbm, fo_hbm,
    res, cot, loc, base, xg, r1, pn, wv, ct, po, ps, pr, cs, nr, ng, dws,
    sq, rcol, sums, inns, fq, fr, fp, fs,
    lsem, ssem, r_sum, r_inn, r_r1, r_pn, r_pd, r_w, r_ct, r_pr, r_nr, r_dw, r_fr, r_fo,
):
    r = lax.axis_index("replica")
    f = lax.axis_index("fsdp")
    t = lax.axis_index("tensor")
    x, c = lax.div(f, 2), lax.rem(f, 2)
    y, zl = lax.div(t, 2), lax.rem(t, 2)

    def dev(x_, c_, y_, z_, r_=r):
        return (r_, x_ * 2 + c_, y_ * 2 + z_)

    def ring(v, o):
        return lax.rem(v + o, 4)

    sib = dev(x, 1 - c, y, zl)
    swap = dev(x, 1 - c, y, 1 - zl)
    rows_of = [dev(x, c, ring(y, o), zl) for o in range(4)]
    xup, xdown, xfar = (dev(ring(x, o), c, y, zl) for o in (1, 3, 2))
    others = [dev(ring(x, o), c, ring(y, p), zl) for o in (1, 2, 3) for p in (1, 2, 3)]
    tensors = [(r, f, lax.rem(t + o, 8)) for o in range(1, 8)]
    replicas = [(ring(r, o), f, t) for o in (1, 2, 3)]
    d = ring(y - x + 4, 0)
    straight = c == zl
    crossed = c != zl

    barrier = pltpu.get_barrier_semaphore()
    peers = tensors + replicas + others + [sib, swap, xup, xdown, xfar]
    for peer in peers:
        pl.semaphore_signal(barrier, inc=1, device_id=peer, device_id_type=MESH)

    loads = [
        pltpu.make_async_copy(src, dst, lsem.at[i])
        for i, (src, dst) in enumerate(((res_hbm, res), (cot_hbm, cot), (loc_hbm, loc), (base_hbm, base)))
    ]
    for load in loads:
        load.start()

    sends = []

    def make(src, dst, sem, device, pred=None):
        cp = pltpu.make_async_remote_copy(
            src_ref=src, dst_ref=dst, send_sem=ssem.at[len(sends)], recv_sem=sem, device_id=device, device_id_type=MESH
        )
        sends.append((pred, cp))
        return cp

    def send(src, dst, sem, device, pred=None):
        cp = make(src, dst, sem, device, pred)
        if pred is None:
            cp.start()
        else:
            pl.when(pred)(cp.start)

    def arrive(ref, sem):
        pltpu.make_async_remote_copy(
            src_ref=ref, dst_ref=ref, send_sem=ssem.at[0], recv_sem=sem, device_id=sib, device_id_type=MESH
        ).wait_recv()

    gain = jnp.concatenate([gain_ref[i : i + 1, :] for i in range(8)], axis=1).astype(F32)

    loads[0].wait()

    def square_rows(i, _):
        rows = pl.ds(pl.multiple_of(i * 32, 32), 32)
        v = res[rows, :].astype(F32)
        sq[rows, :] = lanes(v * v)
        g = (v * gain).astype(BF)
        for m in range(4):
            xg[m, rows, :] = g[:, m * 256 : (m + 1) * 256]
        return 0

    lax.fori_loop(0, TOK // 32, square_rows, 0)
    r1[0] = xg[0]
    sums[t] = jnp.broadcast_to(jnp.sum(sq[...].T, axis=0, keepdims=True), (8, TOK))
    loads[1].wait()

    @pl.when(straight)
    def _():
        ct[x, c] = cot[...]

    def slot(k):
        return ring(x, (0, 1, 3, 2)[k])

    def ct_arrive(xs, cc):
        arrive(ct.at[xs, cc], r_ct.at[xs, cc])

    nxt, prv = replicas[0], replicas[2]

    def half_rows(o, h):
        return pl.ds(pl.multiple_of(ring(r, o) * QROWS + h * 128, 128), 128)

    def frag_send():
        send(fq.at[half_rows(2, 0)], fr.at[0], r_fr.at[0], nxt)
        send(fq.at[half_rows(2, 1)], fr.at[1], r_fr.at[1], prv)
        send(fq.at[half_rows(1, 1)], fr.at[2], r_fr.at[2], nxt)
        send(fq.at[half_rows(3, 0)], fr.at[3], r_fr.at[3], prv)

    pl.semaphore_wait(barrier, len(peers))

    for peer in tensors:
        send(sums.at[t], sums.at[t], r_sum.at[t], peer)

    for m in (1, 3, 2):
        send(xg.at[m], r1.at[m], r_r1.at[m], rows_of[m])

    send(cot, ct.at[x, c], r_ct.at[x, c], dev(x, zl, y, 1 - zl))
    send(cot, ct.at[x, c], r_ct.at[x, c], sib, crossed)
    over = []
    for cc in (c, 1 - c):
        ref = ct.at[x, cc]
        over.append([make(ref, ref, r_ct.at[x, cc], peer) for peer in (xup, xdown)])

    @pl.when(straight)
    def _():
        for cp in over[0]:
            cp.start()

    w_own = [pltpu.make_async_copy(w_hbm.at[pl.ds(q * 256, 256)], wv.at[q], r_w.at[q]) for q in range(4)]

    @pl.when(straight)
    def _():
        for q in range(4):
            w_own[q].start()

    for q in range(4):
        send(w_hbm.at[pl.ds(q * 256, 256)], wv.at[q], r_w.at[q], swap, crossed)

    @pl.when(straight)
    def _():
        ct_arrive(x, 1 - c)
        for cp in over[1]:
            cp.start()

    loads[2].wait()
    loads[3].wait()

    def code_rows(i, _):
        rows = pl.ds(pl.multiple_of(i * 64, 64), 64)
        delta = base[rows, :].astype(F32) - loc[rows, :].astype(F32)
        for l in range(2):
            span = slice(l * BLOCK, (l + 1) * BLOCK)
            block = delta[:, span]
            scale = (jnp.max(jnp.abs(block), axis=-1, keepdims=True) + 1e-06).astype(BF).astype(F32)
            code = (block / scale).astype(BF).astype(F32)
            fq[rows, span] = (code * scale).astype(BF)
        return 0

    lax.fori_loop(0, FEAT // 64, code_rows, 0)

    for o in range(1, 8):
        other = lax.rem(t + o, 8)
        arrive(sums.at[other], r_sum.at[other])
    total = jnp.sum(sums[...], axis=0)[0:1]
    rinv = lax.rsqrt(total / D + EPS)
    rcol[...] = jnp.broadcast_to(rinv, (128, TOK)).T

    xl, xr = ring(x, 3), ring(x, 1)
    hand = [
        make(ct.at[xl, 0], ct.at[xl, 0], r_ct.at[xl, 0], xup),
        make(ct.at[xr, 1], ct.at[xr, 1], r_ct.at[xr, 1], xdown),
    ]

    def hand_on():
        ct_arrive(xl, 0)
        hand[0].start()
        ct_arrive(xr, 1)
        hand[1].start()

    def times_rinv(m):
        by = rcol[...]
        return jnp.concatenate([(r1[m, :, l * 128 : (l + 1) * 128].astype(F32) * by).astype(BF) for l in range(2)], axis=1)

    def columns():
        for m in (1, 3, 2):
            arrive(r1.at[m], r_r1.at[m])
        for o in (1, 3, 2):
            m = ring(d, 4 - o)
            r1[m] = times_rinv(m)
            send(r1.at[m], pn.at[m, x, c], r_pn.at[m, x], dev(ring(x, o), c, y, zl))
        pn[d, x, c] = times_rinv(d)

    def spread(k):
        xs = slot(k)
        ref = pn.at[d, xs, c]
        if k:
            arrive(ref, r_pn.at[d, xs])
        for o in (1, 3, 2):
            send(ref, ref, r_pn.at[d, xs], rows_of[o])

    def quarter(i):
        return ring(d, (0, 1, 3, 2)[i])

    def pair(i):
        m = quarter(i)
        if i:
            for k in range(4):
                arrive(pn.at[m, slot(k), c], r_pn.at[m, slot(k)])
        send(pn.at[m, :, c], pn.at[m, :, c], r_pd.at[m], sib)

    nt = (((1,), (1,)), ((), ()))
    tn = (((0,), (0,)), ((), ()))

    plan = [(0, 0), (0, 1), (0, 2), (1, 0), (1, 1), (1, 2), (0, 3)]
    plan += [(2, 4 + p) for p in range(4)] + [(1, 3)] + [(3, 4 + p) for p in range(4)]

    def offset(j):
        p = plan[j][1]
        if p > 3:
            return ring(y, p - 4)
        if p == 3:
            return 2
        o = lax.rem(y + p, 3)
        return o + lax.div(o, 2)

    def a_start(j):
        q, xs = plan[j][0], ring(x, offset(j))
        right = wv[q]
        ps[j] = lax.dot_general(ct[xs, 1 - c], right, nt, preferred_element_type=F32).astype(BF)
        send(ps.at[j], pr.at[j], r_pr.at[j], sib)
        po[j % 4] = lax.dot_general(ct[xs, c], right, nt, preferred_element_type=F32)

    def a_end(j):
        q, o = plan[j][0], offset(j)
        arrive(pr.at[j], r_pr.at[j])
        total = (po[j % 4] + pr[j].astype(F32)).astype(BF)
        cs[j] = total
        send(cs.at[j], nr.at[y, q], r_nr.at[y, q], dev(ring(x, o), c, x, zl), d + o != 0)

        @pl.when(d + o == 0)
        def _():
            nr[y, q] = total

    w_out = []

    def dw_step(i):
        m = quarter(i)
        arrive(pn.at[m, :, 1 - c], r_pd.at[m])
        left = pn[m].reshape(8 * TOK, 256)
        right = ct[...].reshape(8 * TOK, COLS)
        dws[m] = lax.dot_general(left, right, tn, preferred_element_type=F32).astype(BF)
        rows = pl.ds(pl.multiple_of(m * 256, 256), 256)
        send(dws.at[m], dw_hbm.at[rows], r_dw.at[m], swap, crossed)
        w_out.append(pltpu.make_async_copy(dws.at[m], dw_hbm.at[rows], r_dw.at[m]))
        pl.when(straight)(w_out[i].start)

    mine = pl.ds(pl.multiple_of(r * QROWS, QROWS), QROWS)
    keep = pltpu.make_async_copy(fs, fo_hbm.at[mine], lsem.at[4])

    def frag_pass():
        for h, o, peer in ((0, 1, nxt), (1, 3, prv)):
            arrive(fr.at[h], r_fr.at[h])
            fp[h] = (fr[h].astype(F32) + fq[half_rows(o, h), :].astype(F32)).astype(BF)
            send(fp.at[h], fr.at[4 + h], r_fr.at[4 + h], peer)

    def frag_sum():
        for h in range(2):
            arrive(fr.at[4 + h], r_fr.at[4 + h])
            arrive(fr.at[3 - h], r_fr.at[3 - h])
            v = fq[half_rows(0, h), :].astype(F32) + fr[4 + h].astype(F32) + fr[3 - h].astype(F32)
            fs[pl.ds(h * 128, 128), :] = (v * 0.25).astype(BF)
        keep.start()
        for h in range(2):
            span = pl.ds(h * 128, 128)
            for peer in (nxt, prv):
                send(fs.at[span], fo_hbm.at[half_rows(0, h)], r_fo.at[r, h], peer)

    def frag_forward():
        for h, o, peer in ((0, 3, nxt), (1, 1, prv)):
            ref, sem = fo_hbm.at[half_rows(o, h)], r_fo.at[ring(r, o), h]
            arrive(ref, sem)
            send(ref, ref, sem, peer)

    def w_arrive(q):
        pltpu.make_async_copy(wv.at[q], wv.at[q], r_w.at[q]).wait()

    columns()
    spread(0)
    frag_send()

    @pl.when(crossed)
    def _():
        for cc, cps in zip((c, 1 - c), over):
            ct_arrive(x, cc)
            for cp in cps:
                cp.start()

    pl.when(straight)(hand_on)
    for k in (1, 2, 3):
        spread(k)
    pair(0)
    pl.when(crossed)(hand_on)
    ct_arrive(xr, 0)
    ct_arrive(xl, 1)
    for j in range(16):
        if plan[j] == (0, 3):
            ct_arrive(ring(x, 2), 0)
            ct_arrive(ring(x, 2), 1)
        if j in (0, 3, 7, 12):
            w_arrive(plan[j][0])
        a_start(j)
        if j == 9:
            dw_step(0)
        if j >= LAG:
            a_end(j - LAG)
        if j == 11:
            frag_pass()
        if j == 10:
            pair(1)
        if j == 13:
            dw_step(1)
    for j in range(16 - LAG, 16):
        a_end(j)
    pair(2)
    frag_sum()
    pair(3)
    dw_step(2)
    frag_forward()
    dw_step(3)

    for q in range(4):
        span = slice(q * 256, (q + 1) * 256)
        for p in range(4):
            if p == 0:
                pl.when(d != 0)(lambda q=q: arrive(nr.at[y, q], r_nr.at[y, q]))
            else:
                arrive(nr.at[ring(y, p), q], r_nr.at[ring(y, p), q])

        def inner_rows(i, _):
            rows = pl.ds(pl.multiple_of(i * 32, 32), 32)
            v = nr[0, q, rows, :].astype(F32)
            for p in range(1, 4):
                v = v + nr[p, q, rows, :].astype(F32)
            v = v * gain[:, span]
            ng[rows, span] = v
            v = lanes(v * res[rows, span].astype(F32))
            sq[rows, :] = v if q == 0 else sq[rows, :] + v
            return 0

        lax.fori_loop(0, TOK // 32, inner_rows, 0)
    inns[t] = jnp.broadcast_to(jnp.sum(sq[...].T, axis=0, keepdims=True), (8, TOK))
    for peer in tensors:
        send(inns.at[t], inns.at[t], r_inn.at[t], peer)
    for o in range(1, 8):
        other = lax.rem(t + o, 8)
        arrive(inns.at[other], r_inn.at[other])
    inner = jnp.broadcast_to(jnp.sum(inns[...], axis=0)[0:1] / D, (128, TOK)).T
    sq[...] = rcol[...] * rcol[...] * rcol[...] * inner

    def out_rows(i, _):
        rows = pl.ds(pl.multiple_of(i * 32, 32), 32)
        by, rv = sq[rows, :], rcol[rows, :]
        for l in range(FEAT // 128):
            span = slice(l * 128, (l + 1) * 128)
            rg_ref[rows, span] = (ng[rows, span] * rv - res[rows, span].astype(F32) * by).astype(BF)
        return 0

    lax.fori_loop(0, TOK // 32, out_rows, 0)

    keep.wait()
    for o, h in ((3, 1), (1, 0), (2, 0), (2, 1)):
        arrive(fo_hbm.at[half_rows(o, h)], r_fo.at[ring(r, o), h])
    for i in range(4):
        w_out[i].wait()
    for pred, cp in sends:
        if pred is None:
            cp.wait_send()
        else:
            pl.when(pred)(cp.wait_send)


def finish(dw_ref, outer_ref, base_ref, moment_ref, rg_in, dw_out, frag_out, moment_out, rg_out):
    dw_out[...] = dw_ref[...].astype(F32)
    outer = outer_ref[...].astype(F32)
    moment = 0.9 * moment_ref[...] + outer
    moment_out[...] = moment
    frag_out[...] = (base_ref[...].astype(F32) - 0.7 * (outer + 0.9 * moment)).astype(BF)
    rg_out[...] = rg_in[...]


def local(residual, norm_gain, kv_weight, kv_cotangent, frag_local, frag_base, frag_moment):
    hbm = pl.BlockSpec(memory_space=pl.ANY)
    vmem = pl.BlockSpec(memory_space=pltpu.VMEM)
    dma = pltpu.SemaphoreType.DMA
    residual_grad, weight_grad, outer_grad = pl.pallas_call(
        kernel,
        out_shape=(
            jax.ShapeDtypeStruct((TOK, FEAT), BF),
            jax.ShapeDtypeStruct((FEAT, COLS), BF),
            jax.ShapeDtypeStruct((FEAT, 256), BF),
        ),
        in_specs=[hbm, vmem, hbm, hbm, hbm, hbm],
        out_specs=(vmem, hbm, hbm),
        scratch_shapes=[
            pltpu.VMEM((TOK, FEAT), BF),
            pltpu.VMEM((TOK, COLS), BF),
            pltpu.VMEM((FEAT, 256), BF),
            pltpu.VMEM((FEAT, 256), BF),
            pltpu.VMEM((4, TOK, 256), BF),
            pltpu.VMEM((4, TOK, 256), BF),
            pltpu.VMEM((4, 4, 2, TOK, 256), BF),
            pltpu.VMEM((4, 256, COLS), BF),
            pltpu.VMEM((4, 2, TOK, COLS), BF),
            pltpu.VMEM((4, TOK, 256), F32),
            pltpu.VMEM((16, TOK, 256), BF),
            pltpu.VMEM((16, TOK, 256), BF),
            pltpu.VMEM((16, TOK, 256), BF),
            pltpu.VMEM((4, 4, TOK, 256), BF),
            pltpu.VMEM((TOK, FEAT), F32),
            pltpu.VMEM((4, 256, COLS), BF),
            pltpu.VMEM((TOK, 128), F32),
            pltpu.VMEM((TOK, 128), F32),
            pltpu.VMEM((8, 8, TOK), F32),
            pltpu.VMEM((8, 8, TOK), F32),
            pltpu.VMEM((FEAT, 256), BF),
            pltpu.VMEM((6, 128, 256), BF),
            pltpu.VMEM((2, 128, 256), BF),
            pltpu.VMEM((QROWS, 256), BF),
            dma((5,)),
            dma((NSEND,)),
            dma((8,)),
            dma((8,)),
            dma((4,)),
            dma((4, 4)),
            dma((4,)),
            dma((4,)),
            dma((4, 2)),
            dma((16,)),
            dma((4, 4)),
            dma((4,)),
            dma((6,)),
            dma((4, 2)),
        ],
        compiler_params=pltpu.CompilerParams(
            collective_id=0, has_side_effects=True, vmem_limit_bytes=60 * 2**20
        ),
        cost_estimate=pl.CostEstimate(flops=6442450944, bytes_accessed=10 * 2**20, transcendentals=0),
    )(residual, norm_gain.reshape(8, 128), kv_weight[0], kv_cotangent, frag_local[0], frag_base)
    def rows(n, width):
        return pl.BlockSpec((n, width), lambda i: (i, 0))

    steps = 2
    specs = [rows(FEAT // steps, w) for w in (COLS, 256, 256, 256)] + [rows(TOK // steps, FEAT)]
    weight_grad, frag_new, moment_new, residual_grad = pl.pallas_call(
        finish,
        grid=(steps,),
        out_shape=(
            jax.ShapeDtypeStruct((FEAT, COLS), F32),
            jax.ShapeDtypeStruct((FEAT, 256), BF),
            jax.ShapeDtypeStruct((FEAT, 256), F32),
            jax.ShapeDtypeStruct((TOK, FEAT), BF),
        ),
        in_specs=specs,
        out_specs=(specs[0], specs[1], specs[1], specs[4]),
    )(weight_grad, outer_grad, frag_base, frag_moment, residual_grad)
    return (residual_grad, weight_grad[None], frag_new, moment_new)


def solution(mesh):
    placed = (
        P(("replica", "fsdp"), "tensor"),
        P("tensor"),
        P("replica", "fsdp", "tensor"),
        P(("replica", "fsdp"), "tensor"),
        P("replica", "fsdp", "tensor"),
        P("fsdp", "tensor"),
        P("fsdp", "tensor"),
    )
    return jax.shard_map(
        local,
        mesh=mesh,
        in_specs=placed,
        out_specs=(
            P(("replica", "fsdp"), "tensor"),
            P("replica", "fsdp", "tensor"),
            P("fsdp", "tensor"),
            P("fsdp", "tensor"),
        ),
        check_vma=False,
    )
```
